512 devices in a mesh: row: 32 (over y_lo, z), col: 16 (over y_hi, x, core).
Axes of the slice: x: 4, y: 4 (y_hi: 2, y_lo: 2; y = y_hi * 2 + y_lo), z: 16, core: 2. Of those that a mesh axis runs over, the one named last changes fastest.
Arguments:
- features: bfloat16 [16, 32, 256, 128], P('col', 'row'), may hold values from -6 to 6
- weight: bfloat16 [128, 256], replicated, may hold values from -0.5 to 0.5
- tile_values: bfloat16 [32, 16, 128, 128, 128], P('row', 'col'), may hold values from -0.125 to 0.125
- tile_rows: int32 [32, 16, 128], P('row', 'col'), may hold values from 0 to 31
- tile_cols: int32 [32, 16, 128], P('row', 'col'), may hold values from 0 to 63
- tile_count: int32 [32, 16], P('row', 'col'), may hold values from 1 to 128, as said below
- cotangent: bfloat16 [131072, 256], P(('row', 'col')), may hold values from -6 to 6
Outputs:
- activations: bfloat16 [131072, 256], P(('row', 'col'))
- weight_grad: float32 [128, 256], replicated
- feature_grad: float32 [16, 32, 256, 128], P('col', 'row')
The draws below stay inside these ranges and needn't reach their ends.
Inputs may be any that keep to these rules, and one draw needn't show every extreme that they name: `tile_count`: the slots in use of each block; at least one block uses all 128.
All inputs are finite; a program needn't handle non-finite values.
Results may differ from the reference program's by a relative error of at most 0.03.
Values may be sent and summed in bfloat16 or wider, within the bound.
No kernel may reach another device: no remote copies, remote signals or barrier semaphores. Data moves between devices by JAX's collectives and lax.ppermute only.
A program may use at most 64 MiB of HBM per device.

```python
import math
import jax
import jax.numpy as jnp
from jax import lax

F_IN = 128
HID = 256
TILE = 128
SUB = 256
TILES = 128
NODES = 131072
TR = 32
TC = 64
N_ROW = 32
N_COL = 16


def draw_tile_count(key, part):
    key = jax.random.fold_in(key, 7)
    first, second, third = jax.random.split(key, 3)
    lower = jax.random.randint(first, (N_ROW, N_COL), max(1, TILES // 8), TILES // 2 + 1)
    busy = jax.random.randint(second, (N_ROW, N_COL), 0, 16) == 0
    counts = jnp.where(busy, TILES, lower).reshape(-1)
    chosen = jax.random.randint(third, (), 0, N_ROW * N_COL)
    counts = jnp.where(jnp.arange(N_ROW * N_COL) == chosen, TILES, counts)
    return counts.reshape(N_ROW, N_COL).astype(jnp.int32)


def set_ends(values, key, low, largest):
    shape = values.shape
    place = [jax.random.randint(jax.random.fold_in(key, axis), (), 0, shape[axis]) for axis in range(len(shape))]
    values = values.at[tuple(place)].set(low)
    longest = shape.index(max(shape))
    place[longest] = (place[longest] + 1) % shape[longest]
    return values.at[tuple(place)].set(largest)


def block_scale(own_key, extent, cuts, low, largest):
    gain, own = 1.0, jax.random.fold_in(own_key, 6)
    for axis_at, blocks in cuts:
        steps = jnp.exp(jax.random.uniform(jax.random.fold_in(own, axis_at), (blocks,), jnp.float32, low / len(cuts), largest / len(cuts)))
        gain = gain * jnp.repeat(steps, extent[axis_at] // blocks).reshape([-1 if axis == axis_at else 1 for axis in range(len(extent))])
    return gain


def noise(own_key, shape, scale, most, cuts=(), held_as=jnp.bfloat16):
    loudness = block_scale(own_key, shape, cuts, -0.22, 0.18) if cuts else 1.0
    drawn = jax.random.normal(own_key, shape, jnp.float32) * scale * loudness
    return jnp.minimum(jnp.maximum(drawn, -most), most).astype(held_as)


def setup_inputs(seed: int = 0) -> dict:
    key_of = jax.random.split(jax.random.key(seed), 8)
    features = noise(key_of[0], (N_COL, N_ROW, SUB, F_IN), 1.0, 6.0, ((0, 16), (1, 32)))
    weight = noise(key_of[1], (F_IN, HID), F_IN ** -0.5, 0.5)
    tile_values = noise(key_of[2], (N_ROW, N_COL, TILES, TILE, TILE), (TILE * max(1, TILES // (3 * SUB // TILE))) ** -0.5, 0.125, ((0, 32), (1, 16)))
    tile_rows = set_ends(jax.random.randint(key_of[3], (N_ROW, N_COL, TILES), 0, TR), jax.random.fold_in(key_of[3], 1), 0, TR - 1).astype(jnp.int32)
    tile_cols = set_ends(jax.random.randint(key_of[4], (N_ROW, N_COL, TILES), 0, TC), jax.random.fold_in(key_of[4], 1), 0, TC - 1).astype(jnp.int32)
    tile_count = draw_tile_count(jax.random.fold_in(key_of[7], 71), 0)
    cotangent = noise(key_of[6], (NODES, HID), 1.0, 6.0, ((0, 512),))
    return dict(features=features, weight=weight, tile_values=tile_values, tile_rows=tile_rows, tile_cols=tile_cols, tile_count=tile_count, cotangent=cotangent)


def forward_tiles(values, rows, cols, count, block):
    live = jnp.arange(TILES, dtype=jnp.int32) < count
    values = jnp.where(live[:, None, None], values.astype(jnp.float32), jnp.float32(0.0))
    feats = block.reshape(TC, TILE, F_IN)[cols].astype(jnp.float32)
    prod = jnp.einsum('sij,sjf->sif', values, feats)
    onehot = (rows[:, None] == jnp.arange(TR, dtype=jnp.int32)[None, :]).astype(jnp.float32)
    return jnp.einsum('st,sif->tif', onehot, prod).reshape(TR * TILE, F_IN)

def backward_tiles(values, rows, cols, count, block):
    live = jnp.arange(TILES, dtype=jnp.int32) < count
    values = jnp.where(live[:, None, None], values.astype(jnp.float32), jnp.float32(0.0))
    feats = block.reshape(TR, TILE, F_IN)[rows].astype(jnp.float32)
    prod = jnp.einsum('sij,sif->sjf', values, feats)
    onehot = (cols[:, None] == jnp.arange(TC, dtype=jnp.int32)[None, :]).astype(jnp.float32)
    return jnp.einsum('st,sjf->tjf', onehot, prod).reshape(TC * TILE, F_IN)

def reference(features, weight, tile_values, tile_rows, tile_cols, tile_count, cotangent):
    colblocks = features.reshape(N_COL, N_ROW * SUB, F_IN)

    def row_block(r):

        def step(total, c):
            part = forward_tiles(tile_values[r, c], tile_rows[r, c], tile_cols[r, c], tile_count[r, c], colblocks[c])
            part = lax.optimization_barrier(part.astype(jnp.bfloat16))
            return (total + part.astype(jnp.float32), None)
        total, _ = lax.scan(step, jnp.zeros((N_COL * SUB, F_IN), jnp.float32), jnp.arange(N_COL, dtype=jnp.int32))
        return total.astype(jnp.bfloat16)
    aggregated = lax.map(row_block, jnp.arange(N_ROW, dtype=jnp.int32)).reshape(NODES, F_IN)
    pre = jnp.dot(aggregated, weight, preferred_element_type=jnp.float32)
    activations = jax.nn.silu(pre).astype(jnp.bfloat16)
    sig = jax.nn.sigmoid(pre)
    grad_pre = (cotangent.astype(jnp.float32) * (sig * (1.0 + pre * (1.0 - sig)))).astype(jnp.bfloat16)
    weight_grad = jnp.dot(aggregated.T, grad_pre, preferred_element_type=jnp.float32) * (1.0 / math.sqrt(NODES))
    back = jnp.dot(grad_pre, weight.T, preferred_element_type=jnp.float32).astype(jnp.bfloat16)
    rowblocks = back.reshape(N_ROW, N_COL * SUB, F_IN)

    def col_block(c):

        def step(total, r):
            part = backward_tiles(tile_values[r, c], tile_rows[r, c], tile_cols[r, c], tile_count[r, c], rowblocks[r])
            part = lax.optimization_barrier(part.astype(jnp.bfloat16))
            return (total + part.astype(jnp.float32), None)
        total, _ = lax.scan(step, jnp.zeros((N_ROW * SUB, F_IN), jnp.float32), jnp.arange(N_ROW, dtype=jnp.int32))
        return total
    feature_grad = lax.map(col_block, jnp.arange(N_COL, dtype=jnp.int32)).reshape(N_COL, N_ROW, SUB, F_IN)
    return (activations, weight_grad, feature_grad)
```

```python
import math

import jax
import jax.numpy as jnp
from jax import lax
from jax.experimental import pallas as pl
from jax.experimental.pallas import tpu as pltpu
from jax.sharding import PartitionSpec as P

BF16 = jnp.bfloat16
F32 = jnp.float32
ANY = pl.BlockSpec(memory_space=pl.ANY)
SMEM = pl.BlockSpec(memory_space=pltpu.SMEM)
VMEM = pl.BlockSpec(memory_space=pltpu.VMEM)
VMEM_LIMIT = 32 * 1024 * 1024

N_Y, N_ZH, N_ZL = 2, 4, 4
N_Z = N_ZH * N_ZL
N_PAIR, N_CORE = 8, 2
CHUNK = 16
UNROLL = 4


def shift(x, dy, dz):
    pairs = [
        (y * N_Z + z, (y + dy) % N_Y * N_Z + (z + dz) % N_Z) for y in range(N_Y) for z in range(N_Z)
    ]
    return lax.ppermute(x, "row", pairs)


def swap_cores(x):
    return lax.ppermute(x, "col", [(c, c ^ 1) for c in range(N_PAIR * N_CORE)])


Z_GROUPS = [[y * N_Z + z for z in range(N_Z)] for y in range(N_Y)]
ZH_GROUPS = [
    [y * N_Z + zh * N_ZL + zl for zh in range(N_ZH)] for y in range(N_Y) for zl in range(N_ZL)
]
PAIR_GROUPS = [[p * N_CORE + core for p in range(N_PAIR)] for core in range(N_CORE)]


def exchange(x, axis, groups):
    return lax.all_to_all(x, axis, 0, 0, tiled=True, axis_index_groups=groups)


def copies(x, n):
    return jnp.broadcast_to(x[None], (n,) + x.shape)


def add_up(parts):
    total = parts[0].astype(F32)
    for part in parts[1:]:
        total = total + part.astype(F32)
    return total


def start_tiles(values_hbm, values, sems):
    for c in range(values.shape[0] // CHUNK):
        s = pl.ds(c * CHUNK, CHUNK)
        pltpu.make_async_copy(values_hbm.at[s], values.at[s], sems.at[c]).start()


def each_tile(count, values_hbm, values, sems, step):
    def chunk(c, _):
        s = pl.ds(c * CHUNK, CHUNK)
        pltpu.make_async_copy(values_hbm.at[s], values.at[s], sems.at[c]).wait()
        left = jnp.clip(count - c * CHUNK, 0, CHUNK)

        def body(i, _):
            step(c * CHUNK + i * UNROLL)
            return 0

        lax.fori_loop(0, (left + UNROLL - 1) // UNROLL, body, 0)
        return 0

    lax.fori_loop(0, values.shape[0] // CHUNK, chunk, 0)


def forward_kernel(meta, rows, places, values_hbm, z0, z1, z2, z3, z4, o0, o12, o34, keep, send,
                   values, block, total, value_sems, block_sems):
    start_tiles(values_hbm, values, value_sems)
    q = z0.shape[0]
    moves = [(z0, 0), (z1, q), (z2, 2 * q), (z3, 3 * q), (z4, 3 * q + q // 2), (o0, 4 * q),
             (o12, 5 * q), (o34, 7 * q)]
    moves = [
        pltpu.make_async_copy(src, block.at[pl.ds(at, src.shape[0])], block_sems.at[i])
        for i, (src, at) in enumerate(moves)
    ]
    for move in moves:
        move.start()
    total[...] = jnp.zeros_like(total)
    for move in moves:
        move.wait()
    count = meta[0]
    core = meta[1]
    dump = total.shape[0] - 1

    def step(first):
        products = [
            jnp.dot(values[first + u], block[places[first + u]], preferred_element_type=F32)
            for u in range(UNROLL)
        ]
        for u in range(UNROLL):
            row = jnp.where(first + u < count, rows[first + u], dump)
            total[row] += products[u]

    each_tile(count, values_hbm, values, value_sems, step)
    tile = total.shape[1]
    for p in range(N_PAIR):
        for i in range(2):
            at = pl.ds((2 * p + i) * tile, tile)
            keep[at] = total[(2 * p + core) * 2 + i].astype(BF16)
            send[at] = total[(2 * p + 1 - core) * 2 + i].astype(BF16)


def middle_kernel(parts, weight, cotangent, activations, payload):
    n, sub, width = parts.shape
    aggregated = parts[0].astype(F32)
    for p in range(1, n):
        aggregated = aggregated + parts[p].astype(F32)
    aggregated = aggregated.astype(BF16)
    pre = jnp.dot(aggregated, weight[...], preferred_element_type=F32)
    sig = jax.nn.sigmoid(pre)
    activations[...] = (pre * sig).astype(BF16)
    grad_pre = (cotangent[...].astype(F32) * (sig * (1.0 + pre * (1.0 - sig)))).astype(BF16)
    local = lax.dot_general(
        aggregated, grad_pre, (((0,), (0,)), ((), ())), preferred_element_type=F32
    ).astype(BF16)
    back = lax.dot_general(
        weight[...], grad_pre, (((1,), (1,)), ((), ())), preferred_element_type=F32
    ).astype(BF16)
    share = 2 * width // n
    half = n // 2
    for p in range(n):
        payload[p, :width] = back[:, :width]
        payload[p, width:2 * width] = back[:, width:]
        k = p % half * share
        payload[p, 2 * width:] = local[k:k + share, p // half * width:(p // half + 1) * width]


def backward_kernel(meta, cols, places, values_hbm, mine, other, keep, send,
                    values, block, total, value_sems, block_sems):
    start_tiles(values_hbm, values, value_sems)
    pairs, two = block.shape[1], block.shape[2]
    moves = [
        pltpu.make_async_copy(src.at[:, pl.ds(0, two)], block.at[i], block_sems.at[i])
        for i, src in enumerate((mine, other))
    ]
    for move in moves:
        move.start()
    total[...] = jnp.zeros_like(total)
    for move in moves:
        move.wait()
    count = meta[0]
    my_y = meta[2]
    my_zl = meta[3]
    dump = total.shape[0] - 1
    tile = total.shape[1]

    def step(first):
        products = []
        for u in range(UNROLL):
            at = places[first + u]
            back = block[at // (2 * pairs), at // 2 % pairs, pl.ds(at % 2 * tile, tile)]
            products.append(jnp.dot(back, values[first + u], preferred_element_type=F32))
        for u in range(UNROLL):
            col = jnp.where(first + u < count, cols[first + u], dump)
            total[col] += products[u]

    each_tile(count, values_hbm, values, value_sems, step)
    for d, offset in enumerate((0, 1, 3, 2)):
        zl = (my_zl + offset) % N_ZL
        for zh in range(N_ZH):
            for i in range(2):
                at = pl.ds(((d * N_ZH + zh) * 2 + i) * tile, tile)
                keep[at] = total[(my_y * N_Z + zh * N_ZL + zl) * 2 + i].astype(BF16)
                send[at] = total[((1 - my_y) * N_Z + zh * N_ZL + zl) * 2 + i].astype(BF16)


def on_device(features, weight, tile_values, tile_rows, tile_cols, tile_count, cotangent):
    sub, width = features.shape[2:]
    slots, tile = tile_values.shape[2:4]
    n_row = lax.axis_size("row")
    n_col = lax.axis_size("col")
    assert n_row == N_Y * N_Z and n_col == N_PAIR * N_CORE
    assert tile == width and sub == 2 * tile
    r = lax.axis_index("row")
    c = lax.axis_index("col")
    my_y, my_zl, core = r // N_Z, r % N_ZL, c % N_CORE
    values = tile_values[0, 0]
    rows = tile_rows[0, 0]
    cols = tile_cols[0, 0]
    meta = jnp.stack([tile_count[0, 0], core, my_y, my_zl]).astype(jnp.int32)

    at = cols // 2
    distance = jnp.array([0, 2, 3, 1], jnp.int32)[(at - my_zl) % N_ZL]
    col_places = (
        (((at // N_Z) ^ my_y) * N_ZL + distance) * N_ZH + at // N_ZL % N_ZH
    ) * 2 + cols % 2
    at = rows // 2
    row_places = (((at % N_CORE) ^ core) * N_PAIR + at // N_CORE) * 2 + rows % 2

    z0 = exchange(copies(features[0, 0], N_ZH).reshape(N_ZH * sub, width), "row", ZH_GROUPS)
    half = z0.shape[0] // 2
    z1, z2 = shift(z0, 0, 1), shift(z0, 0, -1)
    z3, z4 = shift(z0[:half], 0, 2), shift(z0[half:], 0, -2)
    o0 = shift(z0, 1, 0)
    o12 = shift(jnp.concatenate([z1, z2]), 1, 0)
    o34 = shift(jnp.concatenate([z3, z4]), 1, 0)
    pieces = [
        piece.reshape(-1, tile, width) for piece in (z0, z1, z2, z3, z4, o0, o12, o34)
    ]
    n_chunks = slots // CHUNK
    rows_n = n_col * sub // tile
    cols_n = n_row * sub // tile
    half_rows = jax.ShapeDtypeStruct((n_col * sub // 2, width), BF16)
    half_cols = jax.ShapeDtypeStruct((n_row * sub // 2, width), BF16)
    flops = 2 * slots * tile * tile * width
    params = pltpu.CompilerParams(vmem_limit_bytes=VMEM_LIMIT)
    keep, send = pl.pallas_call(
        forward_kernel,
        out_shape=(half_rows, half_rows),
        in_specs=[SMEM, SMEM, SMEM] + [ANY] * 9,
        out_specs=(VMEM, VMEM),
        scratch_shapes=[
            pltpu.VMEM((slots, tile, tile), BF16),
            pltpu.VMEM((cols_n, tile, width), BF16),
            pltpu.VMEM((rows_n + 1, tile, width), F32),
            pltpu.SemaphoreType.DMA((n_chunks,)),
            pltpu.SemaphoreType.DMA((len(pieces),)),
        ],
        compiler_params=params,
        cost_estimate=pl.CostEstimate(flops=flops, bytes_accessed=7 << 20, transcendentals=0),
        name="forward_tiles",
    )(meta, rows, col_places, values, *pieces)

    both = (keep.astype(F32) + swap_cores(send).astype(F32)).astype(BF16)
    parts = exchange(both, "col", PAIR_GROUPS).reshape(N_PAIR, sub, width)
    share = 2 * width // N_PAIR
    activations, payload = pl.pallas_call(
        middle_kernel,
        out_shape=(
            jax.ShapeDtypeStruct(cotangent.shape, BF16),
            jax.ShapeDtypeStruct((N_PAIR, sub + share, width), BF16),
        ),
        in_specs=[VMEM] * 3,
        out_specs=(VMEM, VMEM),
        compiler_params=params,
        name="layer",
    )(parts, weight, cotangent)

    mine = exchange(payload.reshape(-1, width), "col", PAIR_GROUPS).reshape(payload.shape)
    other = swap_cores(mine)
    keep, send = pl.pallas_call(
        backward_kernel,
        out_shape=(half_cols, half_cols),
        in_specs=[SMEM, SMEM, SMEM] + [ANY] * 3,
        out_specs=(VMEM, VMEM),
        scratch_shapes=[
            pltpu.VMEM((slots, tile, tile), BF16),
            pltpu.VMEM((N_CORE, N_PAIR, sub, width), BF16),
            pltpu.VMEM((cols_n + 1, tile, width), F32),
            pltpu.SemaphoreType.DMA((n_chunks,)),
            pltpu.SemaphoreType.DMA((N_CORE,)),
        ],
        compiler_params=params,
        cost_estimate=pl.CostEstimate(flops=flops, bytes_accessed=7 << 20, transcendentals=0),
        name="backward_tiles",
    )(meta, cols, row_places, values, mine, other)

    shared = add_up([mine[p, sub:] for p in range(N_PAIR)]) + add_up(
        [other[p, sub:] for p in range(N_PAIR)]
    )
    shared = shared + shift(shared, 1, 0)
    along_z = exchange(copies(shared, N_Z).reshape(-1, width), "row", Z_GROUPS)
    along_z = along_z.reshape(N_Z, share, width)
    shared = add_up([along_z[z] for z in range(N_Z)])
    summed = exchange(copies(shared, N_PAIR).reshape(-1, width), "col", PAIR_GROUPS)
    summed = summed.reshape(2, width, width).transpose(1, 0, 2).reshape(width, 2 * width)
    weight_grad = summed * (1.0 / math.sqrt(sub * n_row * n_col))

    held = (keep.astype(F32) + shift(send, 1, 0).astype(F32)).astype(BF16)
    q = held.shape[0] // N_ZL
    near = shift(held[q:2 * q], 0, 1), shift(held[2 * q:3 * q], 0, -1)
    far = shift(held[3 * q:3 * q + q // 2], 0, 2), shift(held[3 * q + q // 2:], 0, -2)
    held = add_up([held[:q], near[0], near[1], jnp.concatenate(far)]).astype(BF16)
    far = exchange(held, "row", ZH_GROUPS).reshape(N_ZH, 2, width, tile)
    feature_grad = add_up([far[zh] for zh in range(N_ZH)]).transpose(0, 2, 1)
    return activations, weight_grad, feature_grad.reshape(1, 1, sub, width)


def solution(mesh):
    in_specs = (
        P("col", "row", None, None),
        P(),
        P("row", "col", None, None, None),
        P("row", "col", None),
        P("row", "col", None),
        P("row", "col"),
        P(("row", "col"), None),
    )
    out_specs = (P(("row", "col"), None), P(), P("col", "row", None, None))
    return jax.shard_map(
        on_device, mesh=mesh, in_specs=in_specs, out_specs=out_specs, check_vma=False
    )
```

```python
import math

import jax
import jax.numpy as jnp
from jax import lax
from jax.experimental import pallas as pl
from jax.experimental.pallas import tpu as pltpu
from jax.sharding import PartitionSpec as P

BF16 = jnp.bfloat16
F32 = jnp.float32
ANY = pl.BlockSpec(memory_space=pl.ANY)
SMEM = pl.BlockSpec(memory_space=pltpu.SMEM)
VMEM = pl.BlockSpec(memory_space=pltpu.VMEM)
VMEM_LIMIT = 32 * 1024 * 1024

N_Y, N_ZH, N_ZL = 2, 4, 4
N_Z = N_ZH * N_ZL
N_PAIR, N_CORE = 8, 2
UNROLL = 16


def shift(x, dy, dz):
    pairs = [
        (y * N_Z + z, (y + dy) % N_Y * N_Z + (z + dz) % N_Z) for y in range(N_Y) for z in range(N_Z)
    ]
    return lax.ppermute(x, "row", pairs)


def two_along_z(x):
    width = N_PAIR * N_CORE
    pairs = []
    for row in range(N_Y * N_Z):
        for col in range(width):
            z = (row % N_Z + (2 if col % N_CORE else -2)) % N_Z
            pairs.append((row * width + col, (row // N_Z * N_Z + z) * width + col))
    return lax.ppermute(x, ("row", "col"), pairs)


def swap_cores(x):
    return lax.ppermute(x, "col", [(c, c ^ 1) for c in range(N_PAIR * N_CORE)])


Z_GROUPS = [[y * N_Z + z for z in range(N_Z)] for y in range(N_Y)]
ZH_GROUPS = [
    [y * N_Z + zh * N_ZL + zl for zh in range(N_ZH)] for y in range(N_Y) for zl in range(N_ZL)
]
Y_PAIR_GROUPS = [
    [(y * N_Z + z) * N_PAIR * N_CORE + p * N_CORE + core for y in range(N_Y) for p in range(N_PAIR)]
    for z in range(N_Z)
    for core in range(N_CORE)
]
PAIR_GROUPS = [[p * N_CORE + core for p in range(N_PAIR)] for core in range(N_CORE)]


def exchange(x, axis, groups):
    return lax.all_to_all(x, axis, 0, 0, tiled=True, axis_index_groups=groups)


def copies(x, n):
    return jnp.broadcast_to(x[None], (n,) + x.shape)


def add_up(parts):
    total = parts[0].astype(F32)
    for part in parts[1:]:
        total = total + part.astype(F32)
    return total


def load_kernel(values_hbm, values, sem):
    move = pltpu.make_async_copy(values_hbm, values, sem)
    move.start()
    move.wait()


def each_tile(count, step):
    def body(i, _):
        step(i * UNROLL)
        return 0

    lax.fori_loop(0, (count + UNROLL - 1) // UNROLL, body, 0)


def forward_kernel(meta, rows, places, values, both, z1, z2, z3, o3, keep, send,
                   block, total, block_sems):
    q = z3.shape[0]
    moves = [(both, 0), (z1, 2 * q), (z2, 4 * q), (z3, 6 * q), (o3, 7 * q)]
    moves = [
        pltpu.make_async_copy(src, block.at[pl.ds(at, src.shape[0])], block_sems.at[i])
        for i, (src, at) in enumerate(moves)
    ]
    for move in moves:
        move.start()
    total[...] = jnp.zeros_like(total)
    for move in moves:
        move.wait()
    count = meta[0]
    core = meta[1]
    dump = total.shape[0] - 1

    def step(first):
        products = [
            jnp.dot(values[first + u], block[places[first + u]], preferred_element_type=F32)
            for u in range(UNROLL)
        ]
        for u in range(UNROLL):
            row = jnp.where(first + u < count, rows[first + u], dump)
            total[row] += products[u]

    each_tile(count, step)
    tile = total.shape[1]
    for p in range(N_PAIR):
        for i in range(2):
            at = pl.ds((2 * p + i) * tile, tile)
            keep[at] = total[(2 * p + core) * 2 + i].astype(BF16)
            send[at] = total[(2 * p + 1 - core) * 2 + i].astype(BF16)


def middle_kernel(parts, weight, cotangent, activations, payload):
    n, sub, width = parts.shape
    aggregated = parts[0].astype(F32)
    for p in range(1, n):
        aggregated = aggregated + parts[p].astype(F32)
    aggregated = aggregated.astype(BF16)
    pre = jnp.dot(aggregated, weight[...], preferred_element_type=F32)
    sig = jax.nn.sigmoid(pre)
    activations[...] = (pre * sig).astype(BF16)
    grad_pre = (cotangent[...].astype(F32) * (sig * (1.0 + pre * (1.0 - sig)))).astype(BF16)
    local = lax.dot_general(
        aggregated, grad_pre, (((0,), (0,)), ((), ())), preferred_element_type=F32
    ).astype(BF16)
    back = lax.dot_general(
        weight[...], grad_pre, (((1,), (1,)), ((), ())), preferred_element_type=F32
    ).astype(BF16)
    share = 2 * width // n
    half = n // 2
    for p in range(n):
        payload[p, :width] = back[:, :width]
        payload[p, width:2 * width] = back[:, width:]
        k = p % half * share
        payload[p, 2 * width:] = local[k:k + share, p // half * width:(p // half + 1) * width]


def backward_kernel(meta, cols, places, values, mine, other, keep_far, keep_own, send_far, send_own,
                    block, total, block_sems):
    pairs, two = block.shape[1], block.shape[2]
    moves = [
        pltpu.make_async_copy(src.at[:, pl.ds(0, two)], block.at[i], block_sems.at[i])
        for i, src in enumerate((mine, other))
    ]
    for move in moves:
        move.start()
    total[...] = jnp.zeros_like(total)
    for move in moves:
        move.wait()
    count = meta[0]
    my_y = meta[2]
    my_zl = meta[3]
    dump = total.shape[0] - 1
    tile = total.shape[1]

    def step(first):
        products = []
        for u in range(UNROLL):
            at = places[first + u]
            back = block[at // (2 * pairs), at // 2 % pairs, pl.ds(at % 2 * tile, tile)]
            products.append(jnp.dot(back, values[first + u], preferred_element_type=F32))
        for u in range(UNROLL):
            col = jnp.where(first + u < count, cols[first + u], dump)
            total[col] += products[u]

    each_tile(count, step)
    classes = (
        (0, keep_own, send_own, 0),
        (1, keep_far, send_far, 0),
        (3, keep_far, send_far, 1),
        (2, keep_far, send_far, 2),
    )
    for offset, keep, send, place in classes:
        zl = (my_zl + offset) % N_ZL
        for zh in range(N_ZH):
            for i in range(2):
                at = pl.ds(((place * N_ZH + zh) * 2 + i) * tile, tile)
                keep[at] = total[(my_y * N_Z + zh * N_ZL + zl) * 2 + i].astype(BF16)
                send[at] = total[((1 - my_y) * N_Z + zh * N_ZL + zl) * 2 + i].astype(BF16)


def on_device(features, weight, tile_values, tile_rows, tile_cols, tile_count, cotangent):
    sub, width = features.shape[2:]
    slots, tile = tile_values.shape[2:4]
    n_row = lax.axis_size("row")
    n_col = lax.axis_size("col")
    assert n_row == N_Y * N_Z and n_col == N_PAIR * N_CORE
    assert tile == width and sub == 2 * tile
    r = lax.axis_index("row")
    c = lax.axis_index("col")
    my_y, my_zl, core = r // N_Z, r % N_ZL, c % N_CORE
    params = pltpu.CompilerParams(vmem_limit_bytes=VMEM_LIMIT)
    values = pl.pallas_call(
        load_kernel,
        out_shape=jax.ShapeDtypeStruct(tile_values.shape[2:], BF16),
        in_specs=[ANY],
        out_specs=VMEM,
        scratch_shapes=[pltpu.SemaphoreType.DMA],
        compiler_params=params,
        name="load_tiles",
    )(tile_values[0, 0])
    rows = tile_rows[0, 0]
    cols = tile_cols[0, 0]
    meta = jnp.stack([tile_count[0, 0], core, my_y, my_zl]).astype(jnp.int32)

    at = cols // 2
    distance = jnp.array([0, 2, 3, 1], jnp.int32)[(at - my_zl) % N_ZL]
    col_places = (
        (distance * N_Y + ((at // N_Z) ^ my_y)) * N_ZH + at // N_ZL % N_ZH
    ) * 2 + cols % 2
    at = rows // 2
    row_places = (((at % N_CORE) ^ core) * N_PAIR + at // N_CORE) * 2 + rows % 2

    z0 = lax.all_gather(features[0, 0], "row", axis=0, tiled=True, axis_index_groups=ZH_GROUPS)
    o0 = shift(z0, 1, 0)
    z3 = two_along_z(z0)
    both = jnp.concatenate([z0, o0])
    z1, z2 = shift(both, 0, 1), shift(both, 0, -1)
    o3 = shift(z3, 1, 0)
    pieces = [piece.reshape(-1, tile, width) for piece in (both, z1, z2, z3, o3)]
    rows_n = n_col * sub // tile
    cols_n = n_row * sub // tile
    half_rows = jax.ShapeDtypeStruct((n_col * sub // 2, width), BF16)
    one = jax.ShapeDtypeStruct((N_ZH * sub, width), BF16)
    three = jax.ShapeDtypeStruct((3 * N_ZH * sub, width), BF16)
    flops = 2 * slots * tile * tile * width
    keep, send = pl.pallas_call(
        forward_kernel,
        out_shape=(half_rows, half_rows),
        in_specs=[SMEM, SMEM, SMEM, VMEM] + [ANY] * len(pieces),
        out_specs=(VMEM, VMEM),
        scratch_shapes=[
            pltpu.VMEM((cols_n, tile, width), BF16),
            pltpu.VMEM((rows_n + 1, tile, width), F32),
            pltpu.SemaphoreType.DMA((len(pieces),)),
        ],
        compiler_params=params,
        cost_estimate=pl.CostEstimate(flops=flops, bytes_accessed=7 << 20, transcendentals=0),
        name="forward_tiles",
    )(meta, rows, col_places, values, *pieces)

    both = (keep.astype(F32) + swap_cores(send).astype(F32)).astype(BF16)
    parts = exchange(both, "col", PAIR_GROUPS).reshape(N_PAIR, sub, width)
    share = 2 * width // N_PAIR
    activations, payload = pl.pallas_call(
        middle_kernel,
        out_shape=(
            jax.ShapeDtypeStruct(cotangent.shape, BF16),
            jax.ShapeDtypeStruct((N_PAIR, sub + share, width), BF16),
        ),
        in_specs=[VMEM] * 3,
        out_specs=(VMEM, VMEM),
        compiler_params=params,
        name="layer",
    )(parts, weight, cotangent)

    mine = exchange(payload.reshape(-1, width), "col", PAIR_GROUPS).reshape(payload.shape)
    other = swap_cores(mine)
    keep_far, keep_own, send_far, send_own = pl.pallas_call(
        backward_kernel,
        out_shape=(three, one) * 2,
        in_specs=[SMEM, SMEM, SMEM, VMEM] + [ANY] * 2,
        out_specs=(VMEM,) * 4,
        scratch_shapes=[
            pltpu.VMEM((N_CORE, N_PAIR, sub, width), BF16),
            pltpu.VMEM((cols_n + 1, tile, width), F32),
            pltpu.SemaphoreType.DMA((N_CORE,)),
        ],
        compiler_params=params,
        cost_estimate=pl.CostEstimate(flops=flops, bytes_accessed=7 << 20, transcendentals=0),
        name="backward_tiles",
    )(meta, cols, row_places, values, mine, other)

    shared = add_up([mine[p, sub:] for p in range(N_PAIR)]) + add_up(
        [other[p, sub:] for p in range(N_PAIR)]
    )
    send_far, shared = lax.optimization_barrier((send_far, shared))
    across_far, across_own = shift(send_far, 1, 0), shift(send_own, 1, 0)
    along_z = exchange(copies(shared, N_Z).reshape(-1, width), "row", Z_GROUPS)

    held = (keep_far.astype(F32) + across_far.astype(F32)).astype(BF16)
    along_z = along_z.reshape(N_Z, share, width)
    shared = add_up([along_z[z] for z in range(N_Z)])
    q = N_ZH * sub
    far = two_along_z(held[2 * q:])
    near = shift(held[:q], 0, 1), shift(held[q:2 * q], 0, -1)
    summed = exchange(
        copies(shared, N_Y * N_PAIR).reshape(-1, width), ("row", "col"), Y_PAIR_GROUPS
    ).reshape(N_Y, 2, width, width)
    near, far, summed = lax.optimization_barrier((near, far, summed))
    held = add_up([keep_own, across_own, near[0], near[1], far]).astype(BF16)
    far = exchange(held, "row", ZH_GROUPS).reshape(N_ZH, 2, width, tile)
    summed = (summed[0] + summed[1]).transpose(1, 0, 2).reshape(width, 2 * width)
    weight_grad = summed * (1.0 / math.sqrt(sub * n_row * n_col))
    feature_grad = add_up([far[zh] for zh in range(N_ZH)]).transpose(0, 2, 1)
    return activations, weight_grad, feature_grad.reshape(1, 1, sub, width)


def solution(mesh):
    in_specs = (
        P("col", "row", None, None),
        P(),
        P("row", "col", None, None, None),
        P("row", "col", None),
        P("row", "col", None),
        P("row", "col"),
        P(("row", "col"), None),
    )
    out_specs = (P(("row", "col"), None), P(), P("col", "row", None, None))
    return jax.shard_map(
        on_device, mesh=mesh, in_specs=in_specs, out_specs=out_specs, check_vma=False
    )
```

```python
import math

import jax
import jax.numpy as jnp
from jax import lax
from jax.experimental import pallas as pl
from jax.experimental.pallas import tpu as pltpu
from jax.sharding import PartitionSpec as P

BF16 = jnp.bfloat16
F32 = jnp.float32
ANY = pl.BlockSpec(memory_space=pl.ANY)
SMEM = pl.BlockSpec(memory_space=pltpu.SMEM)
VMEM = pl.BlockSpec(memory_space=pltpu.VMEM)
VMEM_LIMIT = 32 * 1024 * 1024

N_Y, N_ZH, N_ZL = 2, 4, 4
N_Z = N_ZH * N_ZL
N_PAIR, N_CORE = 8, 2
UNROLL = 32


def shift(x, dy, dz):
    pairs = [
        (y * N_Z + z, (y + dy) % N_Y * N_Z + (z + dz) % N_Z) for y in range(N_Y) for z in range(N_Z)
    ]
    return lax.ppermute(x, "row", pairs)


def two_along_z(x):
    width = N_PAIR * N_CORE
    pairs = []
    for row in range(N_Y * N_Z):
        for col in range(width):
            z = (row % N_Z + (2 if col % N_CORE else -2)) % N_Z
            pairs.append((row * width + col, (row // N_Z * N_Z + z) * width + col))
    return lax.ppermute(x, ("row", "col"), pairs)


def swap_cores(x):
    return lax.ppermute(x, "col", [(c, c ^ 1) for c in range(N_PAIR * N_CORE)])


Z_GROUPS = [[y * N_Z + z for z in range(N_Z)] for y in range(N_Y)]
ZH_GROUPS = [
    [y * N_Z + zh * N_ZL + zl for zh in range(N_ZH)] for y in range(N_Y) for zl in range(N_ZL)
]
Y_PAIR_GROUPS = [
    [(y * N_Z + z) * N_PAIR * N_CORE + p * N_CORE + core for y in range(N_Y) for p in range(N_PAIR)]
    for z in range(N_Z)
    for core in range(N_CORE)
]
PAIR_GROUPS = [[p * N_CORE + core for p in range(N_PAIR)] for core in range(N_CORE)]


def exchange(x, axis, groups):
    return lax.all_to_all(x, axis, 0, 0, tiled=True, axis_index_groups=groups)


def copies(x, n):
    return jnp.broadcast_to(x[None], (n,) + x.shape)


def add_up(parts):
    total = parts[0].astype(F32)
    for part in parts[1:]:
        total = total + part.astype(F32)
    return total


def load_kernel(values_hbm, values, sem):
    move = pltpu.make_async_copy(values_hbm, values, sem)
    move.start()
    move.wait()


def each_tile(count, step):
    def body(i, _):
        step(i * UNROLL)
        return 0

    lax.fori_loop(0, (count + UNROLL - 1) // UNROLL, body, 0)


def forward_kernel(meta, rows, places, values, both, z1, z2, z3, o3, keep, send,
                   block, total, block_sems):
    q = z3.shape[0]
    moves = [(both, 0), (z1, 2 * q), (z2, 4 * q), (z3, 6 * q), (o3, 7 * q)]
    moves = [
        pltpu.make_async_copy(src, block.at[pl.ds(at, src.shape[0])], block_sems.at[i])
        for i, (src, at) in enumerate(moves)
    ]
    for move in moves:
        move.start()
    total[...] = jnp.zeros_like(total)
    for move in moves:
        move.wait()
    count = meta[0]
    core = meta[1]
    dump = total.shape[0] - 1

    def step(first):
        products = [
            jnp.dot(values[first + u], block[places[first + u]], preferred_element_type=F32)
            for u in range(UNROLL)
        ]
        for u in range(UNROLL):
            row = jnp.where(first + u < count, rows[first + u], dump)
            total[row] += products[u]

    each_tile(count, step)
    tile = total.shape[1]
    for p in range(N_PAIR):
        for i in range(2):
            at = pl.ds((2 * p + i) * tile, tile)
            keep[at] = total[(2 * p + core) * 2 + i].astype(BF16)
            send[at] = total[(2 * p + 1 - core) * 2 + i].astype(BF16)


def middle_kernel(parts, weight, cotangent, activations, payload):
    n, sub, width = parts.shape
    aggregated = parts[0].astype(F32)
    for p in range(1, n):
        aggregated = aggregated + parts[p].astype(F32)
    aggregated = aggregated.astype(BF16)
    pre = jnp.dot(aggregated, weight[...], preferred_element_type=F32)
    sig = jax.nn.sigmoid(pre)
    activations[...] = (pre * sig).astype(BF16)
    grad_pre = (cotangent[...].astype(F32) * (sig * (1.0 + pre * (1.0 - sig)))).astype(BF16)
    local = lax.dot_general(
        aggregated, grad_pre, (((0,), (0,)), ((), ())), preferred_element_type=F32
    ).astype(BF16)
    back = lax.dot_general(
        weight[...], grad_pre, (((1,), (1,)), ((), ())), preferred_element_type=F32
    ).astype(BF16)
    share = 2 * width // n
    half = n // 2
    for p in range(n):
        payload[p, :width] = back[:, :width]
        payload[p, width:2 * width] = back[:, width:]
        k = p % half * share
        payload[p, 2 * width:] = local[k:k + share, p // half * width:(p // half + 1) * width]


def backward_kernel(meta, cols, places, values, mine, other, keep_far, keep_own, send_far, send_own,
                    block, total, block_sems):
    pairs, two = block.shape[1], block.shape[2]
    moves = [
        pltpu.make_async_copy(src.at[:, pl.ds(0, two)], block.at[i], block_sems.at[i])
        for i, src in enumerate((mine, other))
    ]
    for move in moves:
        move.start()
    total[...] = jnp.zeros_like(total)
    for move in moves:
        move.wait()
    count = meta[0]
    my_y = meta[2]
    my_zl = meta[3]
    dump = total.shape[0] - 1
    tile = total.shape[1]

    def step(first):
        products = []
        for u in range(UNROLL):
            at = places[first + u]
            back = block[at // (2 * pairs), at // 2 % pairs, pl.ds(at % 2 * tile, tile)]
            products.append(jnp.dot(back, values[first + u], preferred_element_type=F32))
        for u in range(UNROLL):
            col = jnp.where(first + u < count, cols[first + u], dump)
            total[col] += products[u]

    each_tile(count, step)
    classes = (
        (0, keep_own, send_own, 0),
        (1, keep_far, send_far, 0),
        (3, keep_far, send_far, 1),
        (2, keep_far, send_far, 2),
    )
    for offset, keep, send, place in classes:
        zl = (my_zl + offset) % N_ZL
        for zh in range(N_ZH):
            for i in range(2):
                at = pl.ds(((place * N_ZH + zh) * 2 + i) * tile, tile)
                keep[at] = total[(my_y * N_Z + zh * N_ZL + zl) * 2 + i].astype(BF16)
                send[at] = total[((1 - my_y) * N_Z + zh * N_ZL + zl) * 2 + i].astype(BF16)


def on_device(features, weight, tile_values, tile_rows, tile_cols, tile_count, cotangent):
    sub, width = features.shape[2:]
    slots, tile = tile_values.shape[2:4]
    n_row = lax.axis_size("row")
    n_col = lax.axis_size("col")
    assert n_row == N_Y * N_Z and n_col == N_PAIR * N_CORE
    assert tile == width and sub == 2 * tile
    r = lax.axis_index("row")
    c = lax.axis_index("col")
    my_y, my_zl, core = r // N_Z, r % N_ZL, c % N_CORE
    params = pltpu.CompilerParams(vmem_limit_bytes=VMEM_LIMIT)
    values = pl.pallas_call(
        load_kernel,
        out_shape=jax.ShapeDtypeStruct(tile_values.shape[2:], BF16),
        in_specs=[ANY],
        out_specs=VMEM,
        scratch_shapes=[pltpu.SemaphoreType.DMA],
        compiler_params=params,
        name="load_tiles",
    )(tile_values[0, 0])
    rows = tile_rows[0, 0]
    cols = tile_cols[0, 0]
    meta = jnp.stack([tile_count[0, 0], core, my_y, my_zl]).astype(jnp.int32)

    at = cols // 2
    distance = jnp.array([0, 2, 3, 1], jnp.int32)[(at - my_zl) % N_ZL]
    col_places = (
        (distance * N_Y + ((at // N_Z) ^ my_y)) * N_ZH + at // N_ZL % N_ZH
    ) * 2 + cols % 2
    at = rows // 2
    row_places = (((at % N_CORE) ^ core) * N_PAIR + at // N_CORE) * 2 + rows % 2

    z0 = lax.all_gather(features[0, 0], "row", axis=0, tiled=True, axis_index_groups=ZH_GROUPS)
    o0 = shift(z0, 1, 0)
    z3 = two_along_z(z0)
    both = jnp.concatenate([z0, o0])
    z1, z2 = shift(both, 0, 1), shift(both, 0, -1)
    o3 = shift(z3, 1, 0)
    pieces = [piece.reshape(-1, tile, width) for piece in (both, z1, z2, z3, o3)]
    rows_n = n_col * sub // tile
    cols_n = n_row * sub // tile
    half_rows = jax.ShapeDtypeStruct((n_col * sub // 2, width), BF16)
    one = jax.ShapeDtypeStruct((N_ZH * sub, width), BF16)
    three = jax.ShapeDtypeStruct((3 * N_ZH * sub, width), BF16)
    flops = 2 * slots * tile * tile * width
    keep, send = pl.pallas_call(
        forward_kernel,
        out_shape=(half_rows, half_rows),
        in_specs=[SMEM, SMEM, SMEM, VMEM] + [ANY] * len(pieces),
        out_specs=(VMEM, VMEM),
        scratch_shapes=[
            pltpu.VMEM((cols_n, tile, width), BF16),
            pltpu.VMEM((rows_n + 1, tile, width), F32),
            pltpu.SemaphoreType.DMA((len(pieces),)),
        ],
        compiler_params=params,
        cost_estimate=pl.CostEstimate(flops=flops, bytes_accessed=7 << 20, transcendentals=0),
        name="forward_tiles",
    )(meta, rows, col_places, values, *pieces)

    both = (keep.astype(F32) + swap_cores(send).astype(F32)).astype(BF16)
    parts = exchange(both, "col", PAIR_GROUPS).reshape(N_PAIR, sub, width)
    share = 2 * width // N_PAIR
    activations, payload = pl.pallas_call(
        middle_kernel,
        out_shape=(
            jax.ShapeDtypeStruct(cotangent.shape, BF16),
            jax.ShapeDtypeStruct((N_PAIR, sub + share, width), BF16),
        ),
        in_specs=[VMEM] * 3,
        out_specs=(VMEM, VMEM),
        compiler_params=params,
        name="layer",
    )(parts, weight, cotangent)

    mine = exchange(payload.reshape(-1, width), "col", PAIR_GROUPS).reshape(payload.shape)
    other = swap_cores(mine)
    keep_far, keep_own, send_far, send_own = pl.pallas_call(
        backward_kernel,
        out_shape=(three, one) * 2,
        in_specs=[SMEM, SMEM, SMEM, VMEM] + [ANY] * 2,
        out_specs=(VMEM,) * 4,
        scratch_shapes=[
            pltpu.VMEM((N_CORE, N_PAIR, sub, width), BF16),
            pltpu.VMEM((cols_n + 1, tile, width), F32),
            pltpu.SemaphoreType.DMA((N_CORE,)),
        ],
        compiler_params=params,
        cost_estimate=pl.CostEstimate(flops=flops, bytes_accessed=7 << 20, transcendentals=0),
        name="backward_tiles",
    )(meta, cols, row_places, values, mine, other)

    shared = add_up([mine[p, sub:] for p in range(N_PAIR)]) + add_up(
        [other[p, sub:] for p in range(N_PAIR)]
    )
    send_far, shared = lax.optimization_barrier((send_far, shared))
    across_far, across_own = shift(send_far, 1, 0), shift(send_own, 1, 0)
    along_z = exchange(copies(shared.astype(BF16), N_Z).reshape(-1, width), "row", Z_GROUPS)

    held = (keep_far.astype(F32) + across_far.astype(F32)).astype(BF16)
    along_z = along_z.reshape(N_Z, share, width)
    shared = add_up([along_z[z] for z in range(N_Z)])
    q = N_ZH * sub
    far = two_along_z(held[2 * q:])
    near = shift(held[:q], 0, 1), shift(held[q:2 * q], 0, -1)
    summed = exchange(
        copies(shared.astype(BF16), N_Y * N_PAIR).reshape(-1, width), ("row", "col"), Y_PAIR_GROUPS
    ).reshape(N_Y, 2, width, width)
    near, far, summed = lax.optimization_barrier((near, far, summed))
    held = add_up([keep_own, across_own, near[0], near[1], far]).astype(BF16)
    far = exchange(held, "row", ZH_GROUPS).reshape(N_ZH, 2, width, tile)
    summed = add_up([summed[0], summed[1]]).transpose(1, 0, 2).reshape(width, 2 * width)
    weight_grad = summed * (1.0 / math.sqrt(sub * n_row * n_col))
    feature_grad = add_up([far[zh] for zh in range(N_ZH)]).transpose(0, 2, 1)
    return activations, weight_grad, feature_grad.reshape(1, 1, sub, width)


def solution(mesh):
    in_specs = (
        P("col", "row", None, None),
        P(),
        P("row", "col", None, None, None),
        P("row", "col", None),
        P("row", "col", None),
        P("row", "col"),
        P(("row", "col"), None),
    )
    out_specs = (P(("row", "col"), None), P(), P("col", "row", None, None))
    return jax.shard_map(
        on_device, mesh=mesh, in_specs=in_specs, out_specs=out_specs, check_vma=False
    )
```

```python
import math

import jax
import jax.numpy as jnp
from jax import lax
from jax.experimental import pallas as pl
from jax.experimental.pallas import tpu as pltpu
from jax.sharding import PartitionSpec as P

BF16 = jnp.bfloat16
F32 = jnp.float32
ANY = pl.BlockSpec(memory_space=pl.ANY)
SMEM = pl.BlockSpec(memory_space=pltpu.SMEM)
VMEM = pl.BlockSpec(memory_space=pltpu.VMEM)
VMEM_LIMIT = 32 * 1024 * 1024

N_Y, N_ZH, N_ZL = 2, 4, 4
N_Z = N_ZH * N_ZL
N_PAIR, N_CORE = 8, 2
UNROLL = 32
PREPARE = 8

SLOT_BITS, ROW_BITS, BLOCK_BITS, COL_BITS, OWN_BIT = (0, 7), (7, 4), (11, 6), (17, 6), 23


def field(entry, bits):
    return (entry >> bits[0]) & ((1 << bits[1]) - 1)


def shift(x, dy, dz):
    pairs = [
        (y * N_Z + z, (y + dy) % N_Y * N_Z + (z + dz) % N_Z) for y in range(N_Y) for z in range(N_Z)
    ]
    return lax.ppermute(x, "row", pairs)


def two_along_z(x):
    width = N_PAIR * N_CORE
    pairs = []
    for row in range(N_Y * N_Z):
        for col in range(width):
            z = (row % N_Z + (2 if col % N_CORE else -2)) % N_Z
            pairs.append((row * width + col, (row // N_Z * N_Z + z) * width + col))
    return lax.ppermute(x, ("row", "col"), pairs)


def swap_cores(x):
    return lax.ppermute(x, "col", [(c, c ^ 1) for c in range(N_PAIR * N_CORE)])


Z_GROUPS = [[y * N_Z + z for z in range(N_Z)] for y in range(N_Y)]
ZH_GROUPS = [
    [y * N_Z + zh * N_ZL + zl for zh in range(N_ZH)] for y in range(N_Y) for zl in range(N_ZL)
]
Y_PAIR_GROUPS = [
    [(y * N_Z + z) * N_PAIR * N_CORE + p * N_CORE + core for y in range(N_Y) for p in range(N_PAIR)]
    for z in range(N_Z)
    for core in range(N_CORE)
]
PAIR_GROUPS = [[p * N_CORE + core for p in range(N_PAIR)] for core in range(N_CORE)]


def exchange(x, axis, groups):
    return lax.all_to_all(x, axis, 0, 0, tiled=True, axis_index_groups=groups)


def copies(x, n):
    return jnp.broadcast_to(x[None], (n,) + x.shape)


def add_up(parts):
    total = parts[0].astype(F32)
    for part in parts[1:]:
        total = total + part.astype(F32)
    return total


def prepare_kernel(meta, entries, values_hbm, values, table, sem):
    move = pltpu.make_async_copy(values_hbm, values, sem)
    move.start()
    slots = values.shape[0]
    count = meta[0]

    def body(i, own):
        for u in range(PREPARE):
            k = i * PREPARE + u
            entry = entries[k]
            used = k < count
            mine = entry >> OWN_BIT
            at = jnp.where(mine == 1, own, count - 1 - (k - own))
            table[jnp.where(used, at, slots + u)] = entry
            own = own + jnp.where(used, mine, 0)
        return own

    steps = (count + PREPARE - 1) // PREPARE
    table[slots + PREPARE] = lax.fori_loop(0, steps, body, jnp.int32(0))
    move.wait()


def each_tile(meta, table, slots, owned, product, place, total):
    own = table[slots + PREPARE]
    low, high = (0, own) if owned else (own, meta[0])
    dump = total.shape[0] - 1

    def body(i, _):
        first = low + i * UNROLL
        entries = [table[jnp.minimum(first + u, high - 1)] for u in range(UNROLL)]
        products = [product(entry) for entry in entries]
        for u in range(UNROLL):
            total[jnp.where(first + u < high, place(entries[u]), dump)] += products[u]
        return 0

    lax.fori_loop(0, (high - low + UNROLL - 1) // UNROLL, body, 0)


def forward_part(owned, meta, table, values, block, out, total):
    slots, tile = values.shape[:2]

    def product(entry):
        features = block[field(entry, BLOCK_BITS)]
        return jnp.dot(values[field(entry, SLOT_BITS)], features, preferred_element_type=F32)

    each_tile(meta, table, slots, owned, product, lambda entry: field(entry, ROW_BITS), total)
    for t in range(total.shape[0] - 1):
        out[t * tile:(t + 1) * tile] = total[t].astype(BF16)


def forward_send_kernel(meta, table, values, both, z1, z2, z3, o3, send, block, total, block_sems):
    q = z3.shape[0]
    moves = [(both, 0), (z1, 2 * q), (z2, 4 * q), (z3, 6 * q), (o3, 7 * q)]
    moves = [
        pltpu.make_async_copy(src, block.at[pl.ds(at, src.shape[0])], block_sems.at[i])
        for i, (src, at) in enumerate(moves)
    ]
    for move in moves:
        move.start()
    total[...] = jnp.zeros_like(total)
    for move in moves:
        move.wait()
    forward_part(False, meta, table, values, block, send, total)


def forward_keep_kernel(meta, table, values, block, keep, total):
    total[...] = jnp.zeros_like(total)
    forward_part(True, meta, table, values, block, keep, total)


def middle_kernel(parts, weight, cotangent, activations, payload):
    n, sub, width = parts.shape
    aggregated = parts[0].astype(F32)
    for p in range(1, n):
        aggregated = aggregated + parts[p].astype(F32)
    aggregated = aggregated.astype(BF16)
    pre = jnp.dot(aggregated, weight[...], preferred_element_type=F32)
    sig = jax.nn.sigmoid(pre)
    activations[...] = (pre * sig).astype(BF16)
    grad_pre = (cotangent[...].astype(F32) * (sig * (1.0 + pre * (1.0 - sig)))).astype(BF16)
    local = lax.dot_general(
        aggregated, grad_pre, (((0,), (0,)), ((), ())), preferred_element_type=F32
    ).astype(BF16)
    back = lax.dot_general(
        weight[...], grad_pre, (((1,), (1,)), ((), ())), preferred_element_type=F32
    ).astype(BF16)
    share = 2 * width // n
    half = n // 2
    for p in range(n):
        payload[p, :width] = back[:, :width]
        payload[p, width:2 * width] = back[:, width:]
        k = p % half * share
        payload[p, 2 * width:] = local[k:k + share, p // half * width:(p // half + 1) * width]


def backward_part(owned, meta, table, values, back, total):
    slots, tile = values.shape[:2]

    def product(entry):
        at = field(entry, ROW_BITS)
        part = back[at >> 1, pl.ds((at & 1) * tile, tile)]
        return jnp.dot(part, values[field(entry, SLOT_BITS)], preferred_element_type=F32)

    each_tile(meta, table, slots, owned, product, lambda entry: field(entry, COL_BITS), total)


def backward_own_kernel(meta, table, values, mine, total):
    total[...] = jnp.zeros_like(total)
    backward_part(True, meta, table, values, mine, total)


def backward_other_kernel(meta, table, values, other, owned, keep_far, keep_own, send_far, send_own,
                          total):
    total[...] = owned[...]
    backward_part(False, meta, table, values, other, total)
    my_y, my_zl, tile = meta[2], meta[3], total.shape[1]
    classes = (
        (0, keep_own, send_own, 0),
        (1, keep_far, send_far, 0),
        (3, keep_far, send_far, 1),
        (2, keep_far, send_far, 2),
    )
    for offset, keep, send, place in classes:
        zl = (my_zl + offset) % N_ZL
        for zh in range(N_ZH):
            for i in range(2):
                at = pl.ds(((place * N_ZH + zh) * 2 + i) * tile, tile)
                keep[at] = total[(my_y * N_Z + zh * N_ZL + zl) * 2 + i].astype(BF16)
                send[at] = total[((1 - my_y) * N_Z + zh * N_ZL + zl) * 2 + i].astype(BF16)


def on_device(features, weight, tile_values, tile_rows, tile_cols, tile_count, cotangent):
    sub, width = features.shape[2:]
    slots, tile = tile_values.shape[2:4]
    n_row = lax.axis_size("row")
    n_col = lax.axis_size("col")
    assert n_row == N_Y * N_Z and n_col == N_PAIR * N_CORE
    assert tile == width and sub == 2 * tile
    r = lax.axis_index("row")
    c = lax.axis_index("col")
    my_y, my_zl, core = r // N_Z, r % N_ZL, c % N_CORE
    meta = jnp.stack([tile_count[0, 0], core, my_y, my_zl]).astype(jnp.int32)
    rows, cols = tile_rows[0, 0], tile_cols[0, 0]
    node = cols >> 1
    distance = (node - my_zl) & (N_ZL - 1)
    distance = jnp.where(distance == 0, 0, jnp.where(distance == 3, 1, distance + 1))
    place = (distance * N_Y + ((node // N_Z) ^ my_y)) * N_ZH + ((node // N_ZL) & (N_ZH - 1))
    entries = jnp.arange(slots, dtype=jnp.int32) | (((rows >> 2) * 2 + (rows & 1)) << ROW_BITS[0])
    entries = entries | ((place * 2 + (cols & 1)) << BLOCK_BITS[0]) | (cols << COL_BITS[0])
    entries = entries | ((((rows >> 1) & 1) == core).astype(jnp.int32) << OWN_BIT)
    params = pltpu.CompilerParams(vmem_limit_bytes=VMEM_LIMIT)
    values, table = pl.pallas_call(
        prepare_kernel,
        out_shape=(
            jax.ShapeDtypeStruct(tile_values.shape[2:], BF16),
            jax.ShapeDtypeStruct((slots + 2 * PREPARE,), jnp.int32),
        ),
        in_specs=[SMEM, SMEM, ANY],
        out_specs=(VMEM, SMEM),
        scratch_shapes=[pltpu.SemaphoreType.DMA],
        compiler_params=params,
        name="prepare",
    )(meta, entries, tile_values[0, 0])

    z0 = lax.all_gather(features[0, 0], "row", axis=0, tiled=True, axis_index_groups=ZH_GROUPS)
    o0 = shift(z0, 1, 0)
    z3 = two_along_z(z0)
    both = jnp.concatenate([z0, o0])
    z1, z2 = shift(both, 0, 1), shift(both, 0, -1)
    o3 = shift(z3, 1, 0)
    pieces = [piece.reshape(-1, tile, width) for piece in (both, z1, z2, z3, o3)]
    rows_n = n_col * sub // tile
    cols_n = n_row * sub // tile
    half_rows = jax.ShapeDtypeStruct((n_col * sub // 2, width), BF16)
    one = jax.ShapeDtypeStruct((N_ZH * sub, width), BF16)
    three = jax.ShapeDtypeStruct((3 * N_ZH * sub, width), BF16)
    all_cols = (cols_n + 1, tile, width)
    cost = pl.CostEstimate(flops=slots * tile * tile * width, bytes_accessed=7 << 20, transcendentals=0)
    send, block = pl.pallas_call(
        forward_send_kernel,
        out_shape=(half_rows, jax.ShapeDtypeStruct((cols_n, tile, width), BF16)),
        in_specs=[SMEM, SMEM, VMEM] + [ANY] * len(pieces),
        out_specs=(VMEM, VMEM),
        scratch_shapes=[
            pltpu.VMEM((rows_n // 2 + 1, tile, width), F32),
            pltpu.SemaphoreType.DMA((len(pieces),)),
        ],
        compiler_params=params,
        cost_estimate=cost,
        name="forward_send",
    )(meta, table, values, *pieces)
    keep = pl.pallas_call(
        forward_keep_kernel,
        out_shape=half_rows,
        in_specs=[SMEM, SMEM, VMEM, VMEM],
        out_specs=VMEM,
        scratch_shapes=[pltpu.VMEM((rows_n // 2 + 1, tile, width), F32)],
        compiler_params=params,
        cost_estimate=cost,
        name="forward_keep",
    )(meta, table, values, block)

    both = (keep.astype(F32) + swap_cores(send).astype(F32)).astype(BF16)
    parts = exchange(both, "col", PAIR_GROUPS).reshape(N_PAIR, sub, width)
    share = 2 * width // N_PAIR
    activations, payload = pl.pallas_call(
        middle_kernel,
        out_shape=(
            jax.ShapeDtypeStruct(cotangent.shape, BF16),
            jax.ShapeDtypeStruct((N_PAIR, sub + share, width), BF16),
        ),
        in_specs=[VMEM] * 3,
        out_specs=(VMEM, VMEM),
        compiler_params=params,
        name="layer",
    )(parts, weight, cotangent)

    mine = exchange(payload.reshape(-1, width), "col", PAIR_GROUPS).reshape(payload.shape)
    other = swap_cores(mine)
    owned = pl.pallas_call(
        backward_own_kernel,
        out_shape=jax.ShapeDtypeStruct(all_cols, F32),
        in_specs=[SMEM, SMEM, VMEM, VMEM],
        out_specs=VMEM,
        compiler_params=params,
        cost_estimate=cost,
        name="backward_own",
    )(meta, table, values, mine)
    keep_far, keep_own, send_far, send_own = pl.pallas_call(
        backward_other_kernel,
        out_shape=(three, one) * 2,
        in_specs=[SMEM, SMEM, VMEM, VMEM, VMEM],
        out_specs=(VMEM,) * 4,
        scratch_shapes=[pltpu.VMEM(all_cols, F32)],
        compiler_params=params,
        cost_estimate=cost,
        name="backward_other",
    )(meta, table, values, other, owned)

    shared = add_up([mine[p, sub:] for p in range(N_PAIR)]) + add_up(
        [other[p, sub:] for p in range(N_PAIR)]
    )
    send_far, shared = lax.optimization_barrier((send_far, shared))
    across_far, across_own = shift(send_far, 1, 0), shift(send_own, 1, 0)
    along_z = exchange(copies(shared.astype(BF16), N_Z).reshape(-1, width), "row", Z_GROUPS)

    held = (keep_far.astype(F32) + across_far.astype(F32)).astype(BF16)
    along_z = along_z.reshape(N_Z, share, width)
    shared = add_up([along_z[z] for z in range(N_Z)])
    q = N_ZH * sub
    far = two_along_z(held[2 * q:])
    near = shift(held[:q], 0, 1), shift(held[q:2 * q], 0, -1)
    summed = exchange(
        copies(shared.astype(BF16), N_Y * N_PAIR).reshape(-1, width), ("row", "col"), Y_PAIR_GROUPS
    ).reshape(N_Y, 2, width, width)
    near, far, summed = lax.optimization_barrier((near, far, summed))
    held = add_up([keep_own, across_own, near[0], near[1], far]).astype(BF16)
    far = exchange(held, "row", ZH_GROUPS).reshape(N_ZH, 2, width, tile)
    summed = add_up([summed[0], summed[1]]).transpose(1, 0, 2).reshape(width, 2 * width)
    weight_grad = summed * (1.0 / math.sqrt(sub * n_row * n_col))
    feature_grad = add_up([far[zh] for zh in range(N_ZH)]).transpose(0, 2, 1)
    return activations, weight_grad, feature_grad.reshape(1, 1, sub, width)


def solution(mesh):
    in_specs = (
        P("col", "row", None, None),
        P(),
        P("row", "col", None, None, None),
        P("row", "col", None),
        P("row", "col", None),
        P("row", "col"),
        P(("row", "col"), None),
    )
    out_specs = (P(("row", "col"), None), P(), P("col", "row", None, None))
    return jax.shard_map(
        on_device, mesh=mesh, in_specs=in_specs, out_specs=out_specs, check_vma=False
    )
```
